32 devices in a mesh: dp: 16 (over z, y, x), rep: 2 (over core).
Axes of the slice: x: 2, y: 2, z: 4, core: 2. Of those that a mesh axis runs over, the one named last changes fastest.
Arguments:
- features: bfloat16 [4096, 1024], P(('dp', 'rep')), may hold values from -6 to 6
- cotangent: bfloat16 [4096, 1024], P(('dp', 'rep')), may hold values from -6 to 6
- routes: int32 [4096, 2], P(('dp', 'rep')), may hold values from 0 to 15, all different within a row; in each aligned block of 128 rows (0 to 127, 128 to 255, ...) at most 24 rows name the same one
- route_weights: float32 [4096, 2], P(('dp', 'rep')), may hold values from 0.2 to 1
- counts: int32 [4096], P(('dp', 'rep')), may hold values from 1 to 4
- cross_weight: bfloat16 [1024, 1024], P(('dp', 'rep')), may hold values from -0.1875 to 0.1875
- gate_weight: bfloat16 [1024, 1024], P(('dp', 'rep')), may hold values from -0.1875 to 0.1875
- cross_bias: float32 [1024], replicated, may hold values from -3 to 3
- gate_bias: float32 [1024], replicated, may hold values from -4 to 4
- expert_in: bfloat16 [16, 1024, 2048], P('dp', None, 'rep'), may hold values from -0.1875 to 0.1875
- expert_out: bfloat16 [16, 2048, 1024], P('dp', 'rep'), may hold values from -0.125 to 0.125
Outputs:
- layer_output: bfloat16 [4096, 1024], P(('dp', 'rep'))
- grad_cross_weight: bfloat16 [1024, 1024], P('rep')
- grad_gate_weight: bfloat16 [1024, 1024], P('rep')
- grad_cross_bias: float32 [1024], P('rep')
- grad_gate_bias: float32 [1024], P('rep')
- grad_expert_in: bfloat16 [16, 1024, 2048], P('dp', None, 'rep')
- grad_expert_out: bfloat16 [16, 2048, 1024], P('dp', 'rep')
The draws below stay inside these ranges and needn't reach their ends.
Inputs may be any that keep to these rules, and one draw needn't show every extreme that they name: `routes`: the two experts of a row differ. In the rows of one device (aligned blocks of 128 rows) no expert is named more than 24 times, and in every draw some expert is named exactly 24 times in some block. Every expert is named by some row.
All inputs are finite; a program needn't handle non-finite values.
Results may differ from the reference program's by a relative error of at most 0.02.
Values may be sent and summed in bfloat16 or wider, within the bound.
A program may use at most 128 MiB of HBM per device.

```python
import math
import jax
import jax.numpy as jnp
import numpy as np
from jax import lax

D = 1024
FF = 2048
TOK_DEV = 128
EXPERTS = 16
CAP = 24
TOKENS = 4096
N_DP = 16
N_REP = 2


def touch_ends(entries, stream_key, least, top_value):
    shape = entries.shape
    spot = [jax.random.randint(jax.random.fold_in(stream_key, axis), (), 0, shape[axis]) for axis in range(len(shape))]
    entries = entries.at[tuple(spot)].set(least)
    longest = shape.index(max(shape))
    spot[longest] = (spot[longest] + 1) % shape[longest]
    return entries.at[tuple(spot)].set(top_value)


def shard_levels(rng, dims, shards, least, top_value):
    factor_of, own = 1.0, jax.random.fold_in(rng, 6)
    for dim, blocks in shards:
        steps = jnp.exp(jax.random.uniform(jax.random.fold_in(own, dim), (blocks,), jnp.float32, least / len(shards), top_value / len(shards)))
        factor_of = factor_of * jnp.repeat(steps, dims[dim] // blocks).reshape([-1 if axis == dim else 1 for axis in range(len(dims))])
    return factor_of


def shared_out(rng, own, number, rows, amount, top, bound, skew):
    order = jax.random.permutation(rng, amount)
    crowded, ordinary = portions_of(amount, rows * top, bound, skew, True), portions_of(amount, rows * top, bound, skew, False)
    places = jnp.arange(amount)

    def named(sizes, offset_by):
        used = int((sizes > 0).sum())
        fixed = max(1, used // 4)
        moved = fixed + (places - fixed + offset_by * (used - fixed)) % max(1, amount - fixed)
        return jnp.zeros((amount,), jnp.int32).at[order[jnp.where(places < fixed, places, moved)]].set(jnp.asarray(sizes, jnp.int32))

    sizes = jnp.where(number % 4 == 0, named(crowded, number // 4), named(ordinary, number - number // 4 - 1))
    mixed = jax.random.permutation(jax.random.fold_in(own, 3), amount)
    giver, taker = mixed[0:amount // 2 * 2:2], mixed[1:amount // 2 * 2:2]
    slack = jnp.minimum(sizes[giver] - 1, bound - sizes[taker]) // 2
    slack = jnp.where((giver == order[0]) | (taker == order[0]) | (sizes[taker] == 0), 0, jnp.maximum(slack, 0))
    moved = jax.random.randint(jax.random.fold_in(own, 4), (amount // 2,), 0, 1 << 20) % (slack + 1)
    sizes = sizes.at[giver].add(-moved).at[taker].add(moved)
    labels = jnp.searchsorted(jnp.cumsum(sizes), jnp.arange(rows * top), side="right").astype(jnp.int32)
    table = labels.reshape(top, rows).T
    table = table[jax.random.permutation(jax.random.fold_in(own, 1), rows)]
    offset_by = jax.random.randint(jax.random.fold_in(own, 2), (rows, 1), 0, top)
    return jnp.take_along_axis(table, (jnp.arange(top)[None, :] + offset_by) % top, axis=1)


def portions_of(number_of, total, most, slope, full):
    weights = [(1 << 20) // math.isqrt(grade ** slope) + 1 for grade in range(1, number_of + 1)]
    largest = most if full else min(most, max(-(-total // number_of), total * weights[0] // sum(weights)))
    least = 1 if total - largest >= number_of - 1 else 0
    holding, rest = [largest] + [least] * (number_of - 1), total - largest - least * (number_of - 1)
    while rest > 0:
        candidates = [i for i in range(1, number_of) if holding[i] < largest] or [i for i in range(1, number_of) if holding[i] < most]
        pool, left = sum([weights[i] for i in candidates]), rest
        for i in candidates:
            addition = min(most - holding[i], max(1, left * weights[i] // pool), rest)
            holding[i] = holding[i] + addition
            rest = rest - addition
    return np.array(holding)


def noise(key, shape, scale, limit, split=(), kind=jnp.bfloat16):
    entries = jax.random.normal(key, shape, jnp.float32) * scale
    if len(split) > 0:
        entries = shard_levels(key, shape, split, -0.22, 0.18) * entries
    return jnp.clip(entries, min=-limit, max=limit).astype(kind)


def setup_inputs(seed: int = 0) -> dict:
    key_list = jax.random.split(jax.random.key(seed), 12)
    features = noise(key_list[0], (TOKENS, D), 1.0, 6.0, ((0, 32),))
    cotangent = noise(key_list[1], (TOKENS, D), 1.0, 6.0, ((0, 32),))
    routes_keys = jax.random.split(jax.random.fold_in(key_list[2], 1), TOKENS // TOK_DEV)
    routes_turns = jax.random.permutation(jax.random.fold_in(key_list[2], 3), TOKENS // TOK_DEV)
    routes = jax.vmap(lambda own, number: shared_out(jax.random.fold_in(key_list[2], 2), own, number, TOK_DEV, EXPERTS, 2, CAP, 2))(routes_keys, routes_turns).reshape((TOKENS, 2))
    route_weights = jnp.clip(0.2 + 0.8 * jax.random.uniform(key_list[3], (TOKENS, 2), jnp.float32) ** shard_levels(key_list[3], (TOKENS, 2), ((0, 32),), -0.2, 0.2), 0.2, 1.0)
    counts = touch_ends(jax.random.randint(key_list[4], (TOKENS,), 1, 5), jax.random.fold_in(key_list[4], 1), 1, 4).astype(jnp.int32)
    cross_weight = noise(key_list[5], (D, D), D ** -0.5, 0.1875, ((0, 32),))
    gate_weight = noise(key_list[6], (D, D), D ** -0.5, 0.1875, ((0, 32),))
    cross_bias = noise(key_list[7], (D,), 0.5, 3.0, (), jnp.float32)
    gate_bias = noise(key_list[8], (D,), 1.0, 4.0, (), jnp.float32)
    expert_in = noise(key_list[9], (EXPERTS, D, FF), D ** -0.5, 0.1875, ((0, 16), (2, 2)))
    expert_out = noise(key_list[10], (EXPERTS, FF, D), FF ** -0.5, 0.125, ((0, 16), (1, 2)))
    return {"features": features, "cotangent": cotangent, "routes": routes, "route_weights": route_weights, "counts": counts, "cross_weight": cross_weight, "gate_weight": gate_weight, "cross_bias": cross_bias, "gate_bias": gate_bias, "expert_in": expert_in, "expert_out": expert_out}


def reference(features, cotangent, routes, route_weights, counts, cross_weight, gate_weight, cross_bias, gate_bias, expert_in, expert_out):
    cross_term = jnp.dot(features, cross_weight, preferred_element_type=jnp.float32) + cross_bias
    gate_term = jax.nn.sigmoid(jnp.dot(features, gate_weight, preferred_element_type=jnp.float32) + gate_bias)
    feature_f = features.astype(jnp.float32)
    crossed = (feature_f * cross_term * gate_term + feature_f).astype(jnp.bfloat16)

    blocks = N_DP * N_REP
    width = D
    block_routes = routes.reshape(blocks, 2 * TOK_DEV)
    onehot = (block_routes[:, :, None] == jnp.arange(EXPERTS, dtype=jnp.int32)[None, None, :]).astype(jnp.int32)
    position = jnp.sum((jnp.cumsum(onehot, axis=1) - 1) * onehot, axis=2)
    slot_index = (jnp.arange(blocks, dtype=jnp.int32)[:, None] * CAP + position).reshape(-1).astype(jnp.int32)
    expert_of = routes.reshape(-1).astype(jnp.int32)
    slot_table = jnp.full((EXPERTS, blocks * CAP), -1, jnp.int32)
    slot_table = slot_table.at[expert_of, slot_index].set(jnp.arange(2 * TOKENS, dtype=jnp.int32))

    upstream = 0.05 * counts.astype(jnp.float32)[:, None] * cotangent.astype(jnp.float32)
    out_grad = (route_weights[:, :, None] * upstream[:, None, :]).astype(jnp.bfloat16).reshape(2 * TOKENS, width)

    def per_expert(packed):
        sources, weight_in, weight_out = packed
        filled = sources >= 0
        source = jnp.where(filled, sources, 0).astype(jnp.int32)
        slot_rows = jnp.where(filled[:, None], crossed[source // 2], jnp.zeros((), jnp.bfloat16))
        slot_grads = jnp.where(filled[:, None], out_grad[source], jnp.zeros((), jnp.bfloat16))
        pre_act = jnp.dot(slot_rows, weight_in, preferred_element_type=jnp.float32)
        squash = jax.nn.sigmoid(pre_act)
        hidden = (pre_act * squash).astype(jnp.bfloat16)
        result = jnp.dot(hidden, weight_out, preferred_element_type=jnp.float32).astype(jnp.bfloat16)
        hid_grad = jnp.dot(slot_grads, weight_out.T, preferred_element_type=jnp.float32)
        pre_grad = (hid_grad * squash * (1.0 + pre_act * (1.0 - squash))).astype(jnp.bfloat16)
        back_rows = jnp.dot(pre_grad, weight_in.T, preferred_element_type=jnp.float32).astype(jnp.bfloat16)
        grad_in = jnp.dot(slot_rows.T, pre_grad, preferred_element_type=jnp.float32).astype(jnp.bfloat16)
        grad_out = jnp.dot(hidden.T, slot_grads, preferred_element_type=jnp.float32).astype(jnp.bfloat16)
        return result, back_rows, grad_in, grad_out

    expert_outs, expert_backs, grad_expert_in, grad_expert_out = lax.map(per_expert, (slot_table, expert_in, expert_out))

    slot_flat = (expert_of * (blocks * CAP) + slot_index).astype(jnp.int32)
    out_rows = expert_outs.reshape(-1, width)[slot_flat].reshape(TOKENS, 2, width).astype(jnp.float32)
    layer_output = (crossed.astype(jnp.float32) + jnp.sum(route_weights[:, :, None] * out_rows, axis=1)).astype(jnp.bfloat16)
    back_gathered = expert_backs.reshape(-1, width)[slot_flat].reshape(TOKENS, 2, width).astype(jnp.float32)
    crossed_grad = upstream + jnp.sum(back_gathered, axis=1)
    cross_grad = (crossed_grad * feature_f * gate_term).astype(jnp.bfloat16)
    gate_grad = (crossed_grad * feature_f * cross_term * gate_term * (1.0 - gate_term)).astype(jnp.bfloat16)
    grad_cross_weight = jnp.dot(features.T, cross_grad, preferred_element_type=jnp.float32).astype(jnp.bfloat16)
    grad_gate_weight = jnp.dot(features.T, gate_grad, preferred_element_type=jnp.float32).astype(jnp.bfloat16)
    grad_cross_bias = jnp.sum(cross_grad.astype(jnp.float32), axis=0)
    grad_gate_bias = jnp.sum(gate_grad.astype(jnp.float32), axis=0)
    return (layer_output, grad_cross_weight, grad_gate_weight, grad_cross_bias, grad_gate_bias, grad_expert_in, grad_expert_out)
```

```python
import functools

import jax
import jax.numpy as jnp
from jax import lax
from jax.experimental import pallas as pl
from jax.experimental.pallas import tpu as pltpu
from jax.sharding import PartitionSpec as P

MESH = pl.DeviceIdType.MESH
DMA = pltpu.SemaphoreType.DMA


def flip(index, mask):
    bit = 1
    while bit <= mask:
        if mask & bit:
            index = index + bit * (1 - 2 * ((index // bit) % 2))
        bit *= 2
    return index


def bit_orders(n):
    bits = n.bit_length() - 1
    down = list(range(bits))[::-1]
    turned = down[:1] + down[2:] + down[1:2]
    return down, turned


def greet(me, rep, partners, everyone=0):
    barrier = pltpu.get_barrier_semaphore()
    pl.semaphore_signal(barrier, inc=1, device_id=(me, 1 - rep), device_id_type=MESH)
    count = 1
    if everyone:
        for d in range(1, everyone):
            to = lax.rem(me + d, everyone)
            pl.semaphore_signal(barrier, inc=1, device_id=(to, rep), device_id_type=MESH)
            count += 1
    else:
        for mask in partners:
            pl.semaphore_signal(
                barrier, inc=1, device_id=(flip(me, mask), rep), device_id_type=MESH
            )
            count += 1
    pl.semaphore_wait(barrier, count)


def remote(src, dst, send, recv, to):
    return pltpu.make_async_remote_copy(
        src_ref=src, dst_ref=dst, send_sem=send, recv_sem=recv, device_id=to, device_id_type=MESH
    )


class Spread:
    def __init__(self, n, me, rep, src, dst, sems):
        self.n, self.me, self.rep = n, me, rep
        self.src, self.dst = src, dst
        self.send, self.recv, self.sib_send, self.sib_recv, self.local = sems
        self.started = []

    def start_own(self):
        n, me, rep = self.n, self.me, self.rep
        copy = pltpu.make_async_copy(self.src.at[me], self.dst.at[rep, me], self.local.at[0])
        copy.start()
        self.own = copy
        sib = remote(
            self.src.at[me], self.dst.at[rep, me], self.sib_send.at[0], self.sib_recv.at[0],
            (me, 1 - rep),
        )
        sib.start()
        self.started.append(sib)

    def start_to(self, d):
        n, me, rep = self.n, self.me, self.rep
        to = lax.rem(me + d, n)
        copy = remote(
            self.src.at[to], self.dst.at[rep, me], self.send.at[d], self.recv.at[d], (to, rep)
        )
        copy.start()
        self.started.append(copy)

    def pass_on(self, d):
        n, me, rep = self.n, self.me, self.rep
        origin = lax.rem(me + (n - d), n)
        block = self.dst.at[rep, origin]
        remote(block, block, self.send.at[d], self.recv.at[d], (me, 1 - rep)).wait_recv()
        copy = remote(
            block, block, self.sib_send.at[d], self.sib_recv.at[d], (me, 1 - rep)
        )
        copy.start()
        self.started.append(copy)

    def finish(self):
        n, me, rep = self.n, self.me, self.rep
        self.own.wait()
        for d in range(n):
            block = self.dst.at[1 - rep, lax.rem(me + (n - d), n)]
            remote(
                block, block, self.sib_send.at[d], self.sib_recv.at[d], (me, 1 - rep)
            ).wait_recv()
        for copy in self.started:
            copy.wait_send()


def order_of(n):
    return list(range(1, n))


def gather_kernel(n, cross_ref, gate_ref, grads_ref, cross_full, gate_full, slots, *sems):
    me, rep = lax.axis_index("dp"), lax.axis_index("rep")
    greet(me, rep, (), n)
    spread = Spread(n, me, rep, grads_ref, slots, sems[5:])
    ag_send, ag_recv, sib_send, sib_recv, own = sems[:5]
    sources, fulls, orders = (cross_ref, gate_ref), (cross_full, gate_full), bit_orders(n)
    started, waits = [], []

    def to_sibling(a, mask):
        place = fulls[a].at[flip(me, mask), rep]
        copy = remote(
            sources[a] if mask == 0 else place, place, sib_send.at[a, mask], sib_recv.at[a, mask],
            (me, 1 - rep),
        )
        copy.start()
        started.append(copy)

    def to_partner(a, mask, bit):
        place = fulls[a].at[flip(me, mask), rep]
        got = mask ^ bit
        copy = remote(
            sources[a] if mask == 0 else place, place, ag_send.at[a, got], ag_recv.at[a, got],
            (flip(me, bit), rep),
        )
        copy.start()
        started.append(copy)

    def arrived(a, mask):
        place = fulls[a].at[flip(me, mask), rep]
        remote(
            place, place, ag_send.at[a, mask], ag_recv.at[a, mask], (me, 1 - rep)
        ).wait_recv()

    steps = len(orders[0])
    distances = order_of(n)
    share = -(-len(distances) // max(1, steps))
    held = [[0], [0]]
    for step in range(steps):
        for a in range(2):
            for mask in held[a]:
                to_partner(a, mask, 1 << orders[a][step])
        if step == 0:
            for a in range(2):
                waits.append(pltpu.make_async_copy(sources[a], fulls[a].at[me, rep], own.at[a]))
                waits[-1].start()
                to_sibling(a, 0)
            spread.start_own()
        for d in distances[step * share : (step + 1) * share]:
            spread.start_to(d)
        for a in range(2):
            fresh = [mask ^ (1 << orders[a][step]) for mask in held[a]]
            for mask in fresh:
                arrived(a, mask)
                to_sibling(a, mask)
            held[a] = held[a] + fresh
    for d in distances:
        spread.pass_on(d)
    for a in range(2):
        for mask in range(n):
            place = fulls[a].at[flip(me, mask), 1 - rep]
            remote(
                place, place, sib_send.at[a, mask], sib_recv.at[a, mask], (me, 1 - rep)
            ).wait_recv()
    for copy in waits:
        copy.wait()
    for copy in started:
        copy.wait_send()
    spread.finish()


def spread_kernel(n, src, dst, *sems):
    me, rep = lax.axis_index("dp"), lax.axis_index("rep")
    greet(me, rep, (), n)
    spread = Spread(n, me, rep, src, dst, sems)
    for d in order_of(n):
        spread.start_to(d)
    spread.start_own()
    for d in order_of(n):
        spread.pass_on(d)
    spread.finish()


def return_kernel(n, first, second, out_first, out_second, theirs, mine, *sems):
    me, rep = lax.axis_index("dp"), lax.axis_index("rep")
    greet(me, rep, (), n)
    sib_send, sib_recv, send, recv, local = sems
    started = []
    parts, outs = (first, second), (out_first, out_second)
    distances = order_of(n) + [0]
    for a in range(2):
        for d in distances:
            to = lax.rem(me + d, n)
            copy = remote(
                parts[a].at[1 - rep, to], theirs.at[a, to], sib_send.at[a, d], sib_recv.at[a, d],
                (me, 1 - rep),
            )
            copy.start()
            started.append(copy)
    own = []
    for a in range(2):
        for d in distances:
            to = lax.rem(me + d, n)
            block = theirs.at[a, to]
            remote(
                block, block, sib_send.at[a, d], sib_recv.at[a, d], (me, 1 - rep)
            ).wait_recv()
            mine[a, to] = (
                parts[a][rep, to].astype(jnp.float32) + theirs[a, to].astype(jnp.float32)
            ).astype(jnp.bfloat16)
            if d:
                copy = remote(
                    mine.at[a, to], outs[a].at[me], send.at[a, d], recv.at[a, d], (to, rep)
                )
                copy.start()
                started.append(copy)
            else:
                copy = pltpu.make_async_copy(mine.at[a, me], outs[a].at[me], local.at[a])
                copy.start()
                own.append(copy)
    for copy in own:
        copy.wait()
    for a in range(2):
        for d in order_of(n):
            block = outs[a].at[lax.rem(me + (n - d), n)]
            remote(block, block, send.at[a, d], recv.at[a, d], (me, 1 - rep)).wait_recv()
    for copy in started:
        copy.wait_send()


def reduce_kernel(
    n, cross_ref, gate_ref, bias_ref, cross_out, gate_out, bias_out,
    total, theirs, landed, bias_sum, bias_landed, *sems
):
    me, rep = lax.axis_index("dp"), lax.axis_index("rep")
    steps = n.bit_length() - 1
    greet(me, rep, [1 << b for b in range(steps)])
    sib_send, sib_recv, rs_send, rs_recv, ag_send, ag_recv, b_send, b_recv, own = sems
    parts, outs, orders = (cross_ref, gate_ref), (cross_out, gate_out), bit_orders(n)
    started = []
    f32, bf16 = jnp.float32, jnp.bfloat16

    def send_bias(step, to):
        copy = remote(
            bias_sum.at[step], bias_landed.at[step], b_send.at[step], b_recv.at[step], to
        )
        copy.start()
        started.append(copy)

    def take_bias(step):
        block = bias_landed.at[step]
        remote(block, block, b_send.at[step], b_recv.at[step], (me, 1 - rep)).wait_recv()
        bias_sum[step + 1] = bias_sum[step] + bias_landed[step]

    bias_sum[0] = bias_ref[...]
    send_bias(0, (me, 1 - rep))

    slot_of = [{}, {}]
    for a in range(2):
        masks = list(range(n))
        for step, b in enumerate(orders[a][::-1]):
            masks = [m for m in masks if not m & (1 << b)]
            for m in masks:
                slot_of[a][step, m] = len(slot_of[a])

    def halve(a, step, mask):
        bit = 1 << orders[a][::-1][step]
        at = flip(me, mask)
        slot = slot_of[a][step, mask ^ bit]
        copy = remote(
            total.at[a, at], landed.at[a, slot], rs_send.at[a, slot], rs_recv.at[a, slot],
            (flip(me, bit), rep),
        )
        copy.start()
        started.append(copy)

    def sending_first(a, step, masks):
        if step >= steps:
            return masks
        bit = 1 << orders[a][::-1][step]
        return [m for m in masks if m & bit] + [m for m in masks if not m & bit]

    def maybe_send(a, step, mask):
        if step < steps and mask & (1 << orders[a][::-1][step]):
            halve(a, step, mask)

    todo = [sending_first(a, 0, list(range(n))) for a in range(2)]
    for i in range(n):
        for a in range(2):
            mask = todo[a][i]
            at = flip(me, mask)
            copy = remote(
                parts[a].at[1 - rep, at], theirs.at[a, at], sib_send.at[a, mask],
                sib_recv.at[a, mask], (me, 1 - rep),
            )
            copy.start()
            started.append(copy)
    for i in range(n):
        for a in range(2):
            mask = todo[a][i]
            at = flip(me, mask)
            block = theirs.at[a, at]
            remote(
                block, block, sib_send.at[a, mask], sib_recv.at[a, mask], (me, 1 - rep)
            ).wait_recv()
            total[a, at] = (parts[a][rep, at].astype(f32) + theirs[a, at].astype(f32)).astype(bf16)
            maybe_send(a, 0, mask)
    take_bias(0)

    masks = [list(range(n)), list(range(n))]
    for step in range(steps):
        send_bias(step + 1, (flip(me, 1 << step), rep))
        for a in range(2):
            bit = 1 << orders[a][::-1][step]
            masks[a] = [m for m in masks[a] if not m & bit]
            todo[a] = sending_first(a, step + 1, masks[a])
        for i in range(len(todo[0])):
            for a in range(2):
                mask = todo[a][i]
                at, slot = flip(me, mask), slot_of[a][step, mask]
                block = landed.at[a, slot]
                remote(
                    block, block, rs_send.at[a, slot], rs_recv.at[a, slot], (me, 1 - rep)
                ).wait_recv()
                total[a, at] = (total[a, at].astype(f32) + landed[a, slot].astype(f32)).astype(bf16)
                maybe_send(a, step + 1, mask)
        take_bias(step + 1)
    bias_out[...] = bias_sum[steps + 1]

    held = [[0], [0]]
    waits = []
    for step in range(steps):
        for i in range(len(held[0])):
            for a in range(2):
                mask, bit = held[a][i], 1 << orders[a][step]
                place = outs[a].at[flip(me, mask)]
                copy = remote(
                    total.at[a, me] if mask == 0 else place, place, ag_send.at[a, mask ^ bit],
                    ag_recv.at[a, mask ^ bit], (flip(me, bit), rep),
                )
                copy.start()
                started.append(copy)
        if step == 0:
            for a in range(2):
                waits.append(pltpu.make_async_copy(total.at[a, me], outs[a].at[me], own.at[a]))
                waits[-1].start()
        for a in range(2):
            fresh = [mask ^ (1 << orders[a][step]) for mask in held[a]]
            for mask in fresh:
                place = outs[a].at[flip(me, mask)]
                remote(
                    place, place, ag_send.at[a, mask], ag_recv.at[a, mask], (me, 1 - rep)
                ).wait_recv()
            held[a] = held[a] + fresh
    for copy in waits:
        copy.wait()
    for copy in started:
        copy.wait_send()


ANY = pl.BlockSpec(memory_space=pl.ANY)
VMEM = pl.BlockSpec(memory_space=pltpu.VMEM)


def shape(dims, dtype=jnp.bfloat16):
    return jax.ShapeDtypeStruct(tuple(dims), dtype)


def params(number):
    return pltpu.CompilerParams(
        collective_id=number, has_side_effects=True, vmem_limit_bytes=40 * 1024 * 1024
    )


def body(
    features,
    cotangent,
    routes,
    route_weights,
    counts,
    cross_weight,
    gate_weight,
    cross_bias,
    gate_bias,
    expert_in,
    expert_out,
):
    f32, bf16 = jnp.float32, jnp.bfloat16
    row_count, width = features.shape
    n = lax.axis_size("dp")
    capacity = max(2, 3 * row_count // n)
    slots_n = n * capacity
    shard_rows = cross_weight.shape[0]
    feature_f = features.astype(f32)

    flat_routes = routes.reshape(-1)
    onehot = (flat_routes[:, None] == jnp.arange(n, dtype=jnp.int32)[None, :]).astype(bf16)
    pairs = jnp.arange(2 * row_count, dtype=jnp.int32)
    earlier = (pairs[:, None] > pairs[None, :]).astype(bf16)
    before = jnp.dot(earlier, onehot, preferred_element_type=f32)
    position = jnp.sum(before * onehot.astype(f32), axis=1).astype(jnp.int32)
    slot_index = (flat_routes * capacity + position).reshape(row_count, 2)
    slot_ids = jnp.arange(slots_n, dtype=jnp.int32)
    match = [(slot_index[:, k, None] == slot_ids[None, :]).astype(bf16) for k in range(2)]

    upstream = 0.05 * counts.astype(f32)[:, None] * cotangent.astype(f32)
    both_match = jnp.concatenate(match, axis=0)
    both_grad = jnp.concatenate(
        [(route_weights[:, k, None] * upstream).astype(bf16) for k in range(2)], axis=0
    )

    def to_slots(matches, rows):
        return (
            lax.dot_general(matches, rows, (((0,), (0,)), ((), ())), preferred_element_type=f32)
            .astype(bf16)
            .reshape(n, capacity, width)
        )

    grad_send = to_slots(both_match, both_grad)
    spread_sems = [DMA((n,)), DMA((n,)), DMA((n,)), DMA((n,)), DMA((1,))]
    cross_full, gate_full, slot_grads = pl.pallas_call(
        functools.partial(gather_kernel, n),
        out_shape=(
            shape((n, 2, shard_rows, width)),
            shape((n, 2, shard_rows, width)),
            shape((2, n, capacity, width)),
        ),
        in_specs=[ANY] * 3,
        out_specs=(ANY,) * 3,
        scratch_shapes=[DMA((2, n)), DMA((2, n)), DMA((2, n)), DMA((2, n)), DMA((2,))]
        + spread_sems,
        compiler_params=params(1),
    )(cross_weight, gate_weight, grad_send)

    cross_term = jnp.dot(features, cross_full.reshape(-1, width), preferred_element_type=f32) + cross_bias
    gate_term = jax.nn.sigmoid(
        jnp.dot(features, gate_full.reshape(-1, width), preferred_element_type=f32) + gate_bias
    )
    crossed = (feature_f * cross_term * gate_term + feature_f).astype(bf16)
    row_send = to_slots(match[0] + match[1], crossed)
    slot_rows = pl.pallas_call(
        functools.partial(spread_kernel, n),
        out_shape=shape((2, n, capacity, width)),
        in_specs=[ANY],
        out_specs=ANY,
        scratch_shapes=spread_sems,
        compiler_params=params(2),
    )(row_send)

    rows2 = slot_rows.reshape(2 * slots_n, width)
    grads2 = slot_grads.reshape(2 * slots_n, width)
    weight_in, weight_out = expert_in[0], expert_out[0]
    pre_act = jnp.dot(rows2, weight_in, preferred_element_type=f32)
    squash = jax.nn.sigmoid(pre_act)
    hidden = (pre_act * squash).astype(bf16)
    partial_value = jnp.dot(hidden, weight_out, preferred_element_type=f32).astype(bf16)
    hid_grad = lax.dot_general(
        grads2, weight_out, (((1,), (1,)), ((), ())), preferred_element_type=f32
    )
    pre_grad = (hid_grad * (squash * (1.0 + pre_act * (1.0 - squash)))).astype(bf16)
    back_part = lax.dot_general(
        pre_grad, weight_in, (((1,), (1,)), ((), ())), preferred_element_type=f32
    ).astype(bf16)
    grad_expert_in = lax.dot_general(
        rows2, pre_grad, (((0,), (0,)), ((), ())), preferred_element_type=f32
    ).astype(bf16)[None]
    grad_expert_out = lax.dot_general(
        hidden, grads2, (((0,), (0,)), ((), ())), preferred_element_type=f32
    ).astype(bf16)[None]

    blocks = (2, n, capacity, width)
    back, returned = pl.pallas_call(
        functools.partial(return_kernel, n),
        out_shape=(shape(blocks[1:]),) * 2,
        in_specs=[VMEM] * 2,
        out_specs=(ANY,) * 2,
        scratch_shapes=[pltpu.VMEM(blocks, bf16), pltpu.VMEM(blocks, bf16)]
        + [DMA((2, n))] * 4
        + [DMA((2,))],
        compiler_params=params(3),
    )(back_part.reshape(blocks), partial_value.reshape(blocks))

    def of_row(k, values):
        return jnp.dot(match[k], values.reshape(slots_n, width), preferred_element_type=f32)

    layer_output = (
        crossed.astype(f32)
        + route_weights[:, 0, None] * of_row(0, returned)
        + route_weights[:, 1, None] * of_row(1, returned)
    ).astype(bf16)
    crossed_grad = upstream + of_row(0, back) + of_row(1, back)
    cross_grad = (crossed_grad * feature_f * gate_term).astype(bf16)
    gate_grad = (crossed_grad * feature_f * cross_term * gate_term * (1.0 - gate_term)).astype(bf16)

    def weight_sum(values):
        return (
            lax.dot_general(features, values, (((0,), (0,)), ((), ())), preferred_element_type=f32)
            .astype(bf16)
            .reshape(2, n, -1, width)
        )

    sums = (weight_sum(cross_grad), weight_sum(gate_grad))
    biases = jnp.stack(
        [jnp.sum(cross_grad.astype(f32), axis=0), jnp.sum(gate_grad.astype(f32), axis=0)]
    )
    biases = jnp.concatenate([biases, jnp.zeros((6, width), f32)], axis=0)
    part = sums[0].shape[2]
    steps = n.bit_length() - 1
    grad_cross, grad_gate, bias_total = pl.pallas_call(
        functools.partial(reduce_kernel, n),
        out_shape=(shape((n, part, width)), shape((n, part, width)), shape((8, width), f32)),
        in_specs=[VMEM] * 3,
        out_specs=(ANY, ANY, VMEM),
        scratch_shapes=[
            pltpu.VMEM((2, n, part, width), bf16),
            pltpu.VMEM((2, n, part, width), bf16),
            pltpu.VMEM((2, n, part, width), bf16),
            pltpu.VMEM((steps + 2, 8, width), f32),
            pltpu.VMEM((steps + 1, 8, width), f32),
        ]
        + [DMA((2, n))] * 6
        + [DMA((steps + 1,))] * 2
        + [DMA((2,))],
        compiler_params=params(4),
    )(*sums, biases)
    half = width // 2
    start = lax.axis_index("rep") * half
    bias_half = lax.dynamic_slice_in_dim(bias_total, start, half, axis=1)
    return (
        layer_output,
        grad_cross.reshape(-1, width),
        grad_gate.reshape(-1, width),
        bias_half[0],
        bias_half[1],
        grad_expert_in,
        grad_expert_out,
    )


def solution(mesh):
    return jax.shard_map(
        body,
        mesh=mesh,
        in_specs=(
            P(("dp", "rep"), None),
            P(("dp", "rep"), None),
            P(("dp", "rep"), None),
            P(("dp", "rep"), None),
            P(("dp", "rep")),
            P(("dp", "rep"), None),
            P(("dp", "rep"), None),
            P(),
            P(),
            P("dp", None, "rep"),
            P("dp", "rep", None),
        ),
        out_specs=(
            P(("dp", "rep"), None),
            P("rep", None),
            P("rep", None),
            P("rep"),
            P("rep"),
            P("dp", None, "rep"),
            P("dp", "rep", None),
        ),
        check_vma=False,
    )
```

```python
import functools

import jax
import jax.numpy as jnp
from jax import lax
from jax.experimental import pallas as pl
from jax.experimental.pallas import tpu as pltpu
from jax.sharding import PartitionSpec as P

MESH = pl.DeviceIdType.MESH
DMA = pltpu.SemaphoreType.DMA


def flip(index, mask):
    bit = 1
    while bit <= mask:
        if mask & bit:
            index = index + bit * (1 - 2 * ((index // bit) % 2))
        bit *= 2
    return index


def stream_count(rows, width):
    return 6 if rows * width >= 16 * 1024 and width >= 384 else 2


def streams_of(n, streams, width):
    bits = n.bit_length() - 1
    first, rest = list(range(bits))[::-1][:1], list(range(bits))[::-1][1:]
    pieces = streams // 2
    edges = [-(-width // 128 * p // pieces) * 128 for p in range(pieces)] + [width]
    found = []
    for p in range(pieces):
        for a in range(2):
            turn = (p if pieces > 1 else a) % max(1, len(rest))
            columns = slice(edges[p], edges[p + 1])
            found.append((a, columns, first + rest[turn:] + rest[:turn]))
    return found


def greet(me, rep, partners, everyone=0):
    barrier = pltpu.get_barrier_semaphore()
    pl.semaphore_signal(barrier, inc=1, device_id=(me, 1 - rep), device_id_type=MESH)
    count = 1
    if everyone:
        for d in range(1, everyone):
            to = lax.rem(me + d, everyone)
            pl.semaphore_signal(barrier, inc=1, device_id=(to, rep), device_id_type=MESH)
            count += 1
    else:
        for mask in partners:
            pl.semaphore_signal(
                barrier, inc=1, device_id=(flip(me, mask), rep), device_id_type=MESH
            )
            count += 1
    pl.semaphore_wait(barrier, count)


def remote(src, dst, send, recv, to):
    return pltpu.make_async_remote_copy(
        src_ref=src, dst_ref=dst, send_sem=send, recv_sem=recv, device_id=to, device_id_type=MESH
    )


class Spread:
    def __init__(self, n, me, rep, src, dst, sems):
        self.n, self.me, self.rep = n, me, rep
        self.src, self.dst = src, dst
        self.send, self.recv, self.sib_send, self.sib_recv, self.local = sems
        self.started = []

    def start_own(self):
        n, me, rep = self.n, self.me, self.rep
        copy = pltpu.make_async_copy(self.src.at[me], self.dst.at[rep, me], self.local.at[0])
        copy.start()
        self.own = copy
        sib = remote(
            self.src.at[me], self.dst.at[rep, me], self.sib_send.at[0], self.sib_recv.at[0],
            (me, 1 - rep),
        )
        sib.start()
        self.started.append(sib)

    def start_to(self, d):
        n, me, rep = self.n, self.me, self.rep
        to = lax.rem(me + d, n)
        copy = remote(
            self.src.at[to], self.dst.at[rep, me], self.send.at[d], self.recv.at[d], (to, rep)
        )
        copy.start()
        self.started.append(copy)

    def pass_on(self, d):
        n, me, rep = self.n, self.me, self.rep
        origin = lax.rem(me + (n - d), n)
        block = self.dst.at[rep, origin]
        remote(block, block, self.send.at[d], self.recv.at[d], (me, 1 - rep)).wait_recv()
        copy = remote(
            block, block, self.sib_send.at[d], self.sib_recv.at[d], (me, 1 - rep)
        )
        copy.start()
        self.started.append(copy)

    def finish(self):
        n, me, rep = self.n, self.me, self.rep
        self.own.wait()
        for d in range(n):
            block = self.dst.at[1 - rep, lax.rem(me + (n - d), n)]
            remote(
                block, block, self.sib_send.at[d], self.sib_recv.at[d], (me, 1 - rep)
            ).wait_recv()
        for copy in self.started:
            copy.wait_send()


def order_of(n):
    return list(range(1, n))


def gather_kernel(n, cross_ref, gate_ref, grads_ref, cross_full, gate_full, slots, *sems):
    me, rep = lax.axis_index("dp"), lax.axis_index("rep")
    greet(me, rep, (), n)
    spread = Spread(n, me, rep, grads_ref, slots, sems[5:])
    ag_send, ag_recv, sib_send, sib_recv, own = sems[:5]
    sources, fulls = (cross_ref, gate_ref), (cross_full, gate_full)
    plan = streams_of(n, stream_count(*cross_ref.shape), cross_ref.shape[1])
    orders = [order for _, _, order in plan]
    started, waits = [], []

    def source(q):
        a, columns, _ = plan[q]
        return sources[a].at[:, columns]

    def full(q, row, core):
        a, columns, _ = plan[q]
        return fulls[a].at[row, core, :, columns]

    def to_sibling(a, mask):
        place = full(a, flip(me, mask), rep)
        copy = remote(
            source(a) if mask == 0 else place, place, sib_send.at[a, mask], sib_recv.at[a, mask],
            (me, 1 - rep),
        )
        copy.start()
        started.append(copy)

    def to_partner(a, mask, bit):
        place = full(a, flip(me, mask), rep)
        got = mask ^ bit
        copy = remote(
            source(a) if mask == 0 else place, place, ag_send.at[a, got], ag_recv.at[a, got],
            (flip(me, bit), rep),
        )
        copy.start()
        started.append(copy)

    def arrived(a, mask):
        place = full(a, flip(me, mask), rep)
        remote(
            place, place, ag_send.at[a, mask], ag_recv.at[a, mask], (me, 1 - rep)
        ).wait_recv()

    steps = len(orders[0])
    distances = order_of(n)
    share = -(-len(distances) // max(1, steps))
    held = [[0] for _ in plan]
    for step in range(steps):
        for a in range(len(plan)):
            for mask in held[a]:
                to_partner(a, mask, 1 << orders[a][step])
        if step == 0:
            for a in range(2):
                waits.append(pltpu.make_async_copy(sources[a], fulls[a].at[me, rep], own.at[a]))
                waits[-1].start()
            for a in range(len(plan)):
                to_sibling(a, 0)
            spread.start_own()
        for d in distances[step * share : (step + 1) * share]:
            spread.start_to(d)
        for a in range(len(plan)):
            fresh = [mask ^ (1 << orders[a][step]) for mask in held[a]]
            for mask in fresh:
                arrived(a, mask)
                to_sibling(a, mask)
            held[a] = held[a] + fresh
    for d in distances:
        spread.pass_on(d)
    for a in range(len(plan)):
        for mask in range(n):
            place = full(a, flip(me, mask), 1 - rep)
            remote(
                place, place, sib_send.at[a, mask], sib_recv.at[a, mask], (me, 1 - rep)
            ).wait_recv()
    for copy in waits:
        copy.wait()
    for copy in started:
        copy.wait_send()
    spread.finish()


def spread_kernel(n, src, dst, *sems):
    me, rep = lax.axis_index("dp"), lax.axis_index("rep")
    greet(me, rep, (), n)
    spread = Spread(n, me, rep, src, dst, sems)
    for d in order_of(n):
        spread.start_to(d)
    spread.start_own()
    for d in order_of(n):
        spread.pass_on(d)
    spread.finish()


def return_kernel(n, first, second, out_first, out_second, theirs, mine, *sems):
    me, rep = lax.axis_index("dp"), lax.axis_index("rep")
    greet(me, rep, (), n)
    sib_send, sib_recv, send, recv, local = sems
    started = []
    parts, outs = (first, second), (out_first, out_second)
    distances = order_of(n) + [0]
    for a in range(2):
        for d in distances:
            to = lax.rem(me + d, n)
            copy = remote(
                parts[a].at[1 - rep, to], theirs.at[a, to], sib_send.at[a, d], sib_recv.at[a, d],
                (me, 1 - rep),
            )
            copy.start()
            started.append(copy)
    own = []
    for a in range(2):
        for d in distances:
            to = lax.rem(me + d, n)
            block = theirs.at[a, to]
            remote(
                block, block, sib_send.at[a, d], sib_recv.at[a, d], (me, 1 - rep)
            ).wait_recv()
            mine[a, to] = (
                parts[a][rep, to].astype(jnp.float32) + theirs[a, to].astype(jnp.float32)
            ).astype(jnp.bfloat16)
            if d:
                copy = remote(
                    mine.at[a, to], outs[a].at[me], send.at[a, d], recv.at[a, d], (to, rep)
                )
                copy.start()
                started.append(copy)
            else:
                copy = pltpu.make_async_copy(mine.at[a, me], outs[a].at[me], local.at[a])
                copy.start()
                own.append(copy)
    for copy in own:
        copy.wait()
    for a in range(2):
        for d in order_of(n):
            block = outs[a].at[lax.rem(me + (n - d), n)]
            remote(block, block, send.at[a, d], recv.at[a, d], (me, 1 - rep)).wait_recv()
    for copy in started:
        copy.wait_send()


def reduce_kernel(
    n, cross_ref, gate_ref, bias_ref, cross_out, gate_out, bias_out,
    total, theirs, landed, bias_sum, bias_landed, *sems
):
    me, rep = lax.axis_index("dp"), lax.axis_index("rep")
    steps = n.bit_length() - 1
    greet(me, rep, [1 << b for b in range(steps)])
    sib_send, sib_recv, rs_send, rs_recv, ag_send, ag_recv, b_send, b_recv, own = sems
    parts, outs = (cross_ref, gate_ref), (cross_out, gate_out)
    plan = streams_of(n, stream_count(*cross_ref.shape[2:]), cross_ref.shape[3])
    orders = [order for _, _, order in plan]
    many = range(len(plan))
    started = []

    def held_at(q, row):
        a, columns, _ = plan[q]
        return total.at[a, row, :, columns]

    def landed_at(q, slot):
        a, columns, _ = plan[q]
        return landed.at[a, slot, :, columns]

    def out_at(q, row):
        a, columns, _ = plan[q]
        return outs[a].at[row, :, columns]
    f32, bf16 = jnp.float32, jnp.bfloat16

    def send_bias(step, to):
        copy = remote(
            bias_sum.at[step], bias_landed.at[step], b_send.at[step], b_recv.at[step], to
        )
        copy.start()
        started.append(copy)

    def take_bias(step):
        block = bias_landed.at[step]
        remote(block, block, b_send.at[step], b_recv.at[step], (me, 1 - rep)).wait_recv()
        bias_sum[step + 1] = bias_sum[step] + bias_landed[step]

    bias_sum[0] = bias_ref[...]
    send_bias(0, (me, 1 - rep))

    slot_of = [{} for _ in many]
    for a in many:
        masks = list(range(n))
        for step, b in enumerate(orders[a][::-1]):
            masks = [m for m in masks if not m & (1 << b)]
            for m in masks:
                slot_of[a][step, m] = len(slot_of[a])

    def halve(a, step, mask):
        bit = 1 << orders[a][::-1][step]
        at = flip(me, mask)
        slot = slot_of[a][step, mask ^ bit]
        copy = remote(
            held_at(a, at), landed_at(a, slot), rs_send.at[a, slot], rs_recv.at[a, slot],
            (flip(me, bit), rep),
        )
        copy.start()
        started.append(copy)

    def sending_first(a, step, masks):
        if step >= steps:
            return masks
        bit = 1 << orders[a][::-1][step]
        return [m for m in masks if m & bit] + [m for m in masks if not m & bit]

    def maybe_send(a, step, mask):
        if step < steps and mask & (1 << orders[a][::-1][step]):
            halve(a, step, mask)

    for mask in reversed(range(n)):
        for a in range(2):
            at = flip(me, mask)
            copy = remote(
                parts[a].at[1 - rep, at], theirs.at[a, at], sib_send.at[a, mask],
                sib_recv.at[a, mask], (me, 1 - rep),
            )
            copy.start()
            started.append(copy)
    for mask in reversed(range(n)):
        at = flip(me, mask)
        for a in range(2):
            block = theirs.at[a, at]
            remote(
                block, block, sib_send.at[a, mask], sib_recv.at[a, mask], (me, 1 - rep)
            ).wait_recv()
            total[a, at] = (parts[a][rep, at].astype(f32) + theirs[a, at].astype(f32)).astype(bf16)
            for q in many:
                if plan[q][0] == a:
                    maybe_send(q, 0, mask)
    take_bias(0)

    masks = [list(range(n)) for _ in many]
    todo = [None for _ in many]
    for step in range(steps):
        send_bias(step + 1, (flip(me, 1 << step), rep))
        for a in many:
            bit = 1 << orders[a][::-1][step]
            masks[a] = [m for m in masks[a] if not m & bit]
            todo[a] = sending_first(a, step + 1, masks[a])
        for i in range(len(todo[0])):
            for a in many:
                mask = todo[a][i]
                at, slot = flip(me, mask), slot_of[a][step, mask]
                block = landed_at(a, slot)
                remote(
                    block, block, rs_send.at[a, slot], rs_recv.at[a, slot], (me, 1 - rep)
                ).wait_recv()
                into = held_at(a, at)
                into[...] = (into[...].astype(f32) + block[...].astype(f32)).astype(bf16)
                maybe_send(a, step + 1, mask)
        take_bias(step + 1)
    bias_out[...] = bias_sum[steps + 1]

    held = [[0] for _ in many]
    waits = []
    for step in range(steps):
        for i in range(len(held[0])):
            for a in many:
                mask, bit = held[a][i], 1 << orders[a][step]
                place = out_at(a, flip(me, mask))
                copy = remote(
                    held_at(a, me) if mask == 0 else place, place, ag_send.at[a, mask ^ bit],
                    ag_recv.at[a, mask ^ bit], (flip(me, bit), rep),
                )
                copy.start()
                started.append(copy)
        if step == 0:
            for a in range(2):
                waits.append(pltpu.make_async_copy(total.at[a, me], outs[a].at[me], own.at[a]))
                waits[-1].start()
        for a in many:
            fresh = [mask ^ (1 << orders[a][step]) for mask in held[a]]
            for mask in fresh:
                place = out_at(a, flip(me, mask))
                remote(
                    place, place, ag_send.at[a, mask], ag_recv.at[a, mask], (me, 1 - rep)
                ).wait_recv()
            held[a] = held[a] + fresh
    for copy in waits:
        copy.wait()
    for copy in started:
        copy.wait_send()


ANY = pl.BlockSpec(memory_space=pl.ANY)
VMEM = pl.BlockSpec(memory_space=pltpu.VMEM)


def shape(dims, dtype=jnp.bfloat16):
    return jax.ShapeDtypeStruct(tuple(dims), dtype)


def params(number):
    return pltpu.CompilerParams(
        collective_id=number, has_side_effects=True, vmem_limit_bytes=40 * 1024 * 1024
    )


def body(
    features,
    cotangent,
    routes,
    route_weights,
    counts,
    cross_weight,
    gate_weight,
    cross_bias,
    gate_bias,
    expert_in,
    expert_out,
):
    f32, bf16 = jnp.float32, jnp.bfloat16
    row_count, width = features.shape
    n = lax.axis_size("dp")
    capacity = max(2, 3 * row_count // n)
    slots_n = n * capacity
    shard_rows = cross_weight.shape[0]
    feature_f = features.astype(f32)

    flat_routes = routes.reshape(-1)
    onehot = (flat_routes[:, None] == jnp.arange(n, dtype=jnp.int32)[None, :]).astype(bf16)
    pairs = jnp.arange(2 * row_count, dtype=jnp.int32)
    earlier = (pairs[:, None] > pairs[None, :]).astype(bf16)
    before = jnp.dot(earlier, onehot, preferred_element_type=f32)
    position = jnp.sum(before * onehot.astype(f32), axis=1).astype(jnp.int32)
    slot_index = (flat_routes * capacity + position).reshape(row_count, 2)
    slot_ids = jnp.arange(slots_n, dtype=jnp.int32)
    match = [(slot_index[:, k, None] == slot_ids[None, :]).astype(bf16) for k in range(2)]

    upstream = 0.05 * counts.astype(f32)[:, None] * cotangent.astype(f32)
    both_match = jnp.concatenate(match, axis=0)
    both_grad = jnp.concatenate(
        [(route_weights[:, k, None] * upstream).astype(bf16) for k in range(2)], axis=0
    )

    def to_slots(matches, rows):
        return (
            lax.dot_general(matches, rows, (((0,), (0,)), ((), ())), preferred_element_type=f32)
            .astype(bf16)
            .reshape(n, capacity, width)
        )

    grad_send = to_slots(both_match, both_grad)
    spread_sems = [DMA((n,)), DMA((n,)), DMA((n,)), DMA((n,)), DMA((1,))]
    cross_full, gate_full, slot_grads = pl.pallas_call(
        functools.partial(gather_kernel, n),
        out_shape=(
            shape((n, 2, shard_rows, width)),
            shape((n, 2, shard_rows, width)),
            shape((2, n, capacity, width)),
        ),
        in_specs=[ANY] * 3,
        out_specs=(ANY,) * 3,
        scratch_shapes=[DMA((stream_count(shard_rows, width), n))] * 4 + [DMA((2,))] + spread_sems,
        compiler_params=params(1),
    )(cross_weight, gate_weight, grad_send)

    cross_term = jnp.dot(features, cross_full.reshape(-1, width), preferred_element_type=f32) + cross_bias
    gate_term = jax.nn.sigmoid(
        jnp.dot(features, gate_full.reshape(-1, width), preferred_element_type=f32) + gate_bias
    )
    crossed = (feature_f * cross_term * gate_term + feature_f).astype(bf16)
    row_send = to_slots(match[0] + match[1], crossed)
    slot_rows = pl.pallas_call(
        functools.partial(spread_kernel, n),
        out_shape=shape((2, n, capacity, width)),
        in_specs=[ANY],
        out_specs=ANY,
        scratch_shapes=spread_sems,
        compiler_params=params(2),
    )(row_send)

    rows2 = slot_rows.reshape(2 * slots_n, width)
    grads2 = slot_grads.reshape(2 * slots_n, width)
    weight_in, weight_out = expert_in[0], expert_out[0]
    pre_act = jnp.dot(rows2, weight_in, preferred_element_type=f32)
    squash = jax.nn.sigmoid(pre_act)
    hidden = (pre_act * squash).astype(bf16)
    partial_value = jnp.dot(hidden, weight_out, preferred_element_type=f32).astype(bf16)
    hid_grad = lax.dot_general(
        grads2, weight_out, (((1,), (1,)), ((), ())), preferred_element_type=f32
    )
    pre_grad = (hid_grad * (squash * (1.0 + pre_act * (1.0 - squash)))).astype(bf16)
    back_part = lax.dot_general(
        pre_grad, weight_in, (((1,), (1,)), ((), ())), preferred_element_type=f32
    ).astype(bf16)
    grad_expert_in = lax.dot_general(
        rows2, pre_grad, (((0,), (0,)), ((), ())), preferred_element_type=f32
    ).astype(bf16)[None]
    grad_expert_out = lax.dot_general(
        hidden, grads2, (((0,), (0,)), ((), ())), preferred_element_type=f32
    ).astype(bf16)[None]

    blocks = (2, n, capacity, width)
    back, returned = pl.pallas_call(
        functools.partial(return_kernel, n),
        out_shape=(shape(blocks[1:]),) * 2,
        in_specs=[VMEM] * 2,
        out_specs=(ANY,) * 2,
        scratch_shapes=[pltpu.VMEM(blocks, bf16), pltpu.VMEM(blocks, bf16)]
        + [DMA((2, n))] * 4
        + [DMA((2,))],
        compiler_params=params(3),
    )(back_part.reshape(blocks), partial_value.reshape(blocks))

    def of_row(k, values):
        return jnp.dot(match[k], values.reshape(slots_n, width), preferred_element_type=f32)

    layer_output = (
        crossed.astype(f32)
        + route_weights[:, 0, None] * of_row(0, returned)
        + route_weights[:, 1, None] * of_row(1, returned)
    ).astype(bf16)
    crossed_grad = upstream + of_row(0, back) + of_row(1, back)
    cross_grad = (crossed_grad * feature_f * gate_term).astype(bf16)
    gate_grad = (crossed_grad * feature_f * cross_term * gate_term * (1.0 - gate_term)).astype(bf16)

    def weight_sum(values):
        return (
            lax.dot_general(features, values, (((0,), (0,)), ((), ())), preferred_element_type=f32)
            .astype(bf16)
            .reshape(2, n, -1, width)
        )

    sums = (weight_sum(cross_grad), weight_sum(gate_grad))
    biases = jnp.stack(
        [jnp.sum(cross_grad.astype(f32), axis=0), jnp.sum(gate_grad.astype(f32), axis=0)]
    )
    biases = jnp.concatenate([biases, jnp.zeros((6, width), f32)], axis=0)
    part = sums[0].shape[2]
    steps = n.bit_length() - 1
    grad_cross, grad_gate, bias_total = pl.pallas_call(
        functools.partial(reduce_kernel, n),
        out_shape=(shape((n, part, width)), shape((n, part, width)), shape((8, width), f32)),
        in_specs=[VMEM] * 3,
        out_specs=(ANY, ANY, VMEM),
        scratch_shapes=[
            pltpu.VMEM((2, n, part, width), bf16),
            pltpu.VMEM((2, n, part, width), bf16),
            pltpu.VMEM((2, n, part, width), bf16),
            pltpu.VMEM((steps + 2, 8, width), f32),
            pltpu.VMEM((steps + 1, 8, width), f32),
        ]
        + [DMA((2, n))] * 2
        + [DMA((stream_count(part, width), n))] * 4
        + [DMA((steps + 1,))] * 2
        + [DMA((2,))],
        compiler_params=params(4),
    )(*sums, biases)
    half = width // 2
    start = lax.axis_index("rep") * half
    bias_half = lax.dynamic_slice_in_dim(bias_total, start, half, axis=1)
    return (
        layer_output,
        grad_cross.reshape(-1, width),
        grad_gate.reshape(-1, width),
        bias_half[0],
        bias_half[1],
        grad_expert_in,
        grad_expert_out,
    )


def solution(mesh):
    return jax.shard_map(
        body,
        mesh=mesh,
        in_specs=(
            P(("dp", "rep"), None),
            P(("dp", "rep"), None),
            P(("dp", "rep"), None),
            P(("dp", "rep"), None),
            P(("dp", "rep")),
            P(("dp", "rep"), None),
            P(("dp", "rep"), None),
            P(),
            P(),
            P("dp", None, "rep"),
            P("dp", "rep", None),
        ),
        out_specs=(
            P(("dp", "rep"), None),
            P("rep", None),
            P("rep", None),
            P("rep"),
            P("rep"),
            P("dp", None, "rep"),
            P("dp", "rep", None),
        ),
        check_vma=False,
    )
```
